256 devices in a mesh: dp: 8 (over z_hi, core), expert: 32 (over z_lo, x, y).
Axes of the slice: x: 4, y: 4, z: 8 (z_hi: 4, z_lo: 2; z = z_hi * 2 + z_lo), core: 2. Of those that a mesh axis runs over, the one named last changes fastest.
Arguments:
- tokens: bfloat16 [4096, 4096], P('expert', 'dp'), may hold values from -6 to 6
- gates: float32 [4096, 8], P('expert'), may hold values from 0.03 to 0.5
- expert_ids: int32 [4096, 8], P('expert'), may hold values from 0 to 31, as said below
- d_mixed: bfloat16 [4096, 4096], P('expert', 'dp'), may hold values from -6 to 6
- w_up: bfloat16 [32, 4096, 1024], P('expert', 'dp'), may hold values from -0.09375 to 0.09375
- w_down: bfloat16 [32, 1024, 4096], P('expert', None, 'dp'), may hold values from -0.1875 to 0.1875
Outputs:
- mixed: bfloat16 [4096, 4096], P('expert', 'dp')
- d_tokens: bfloat16 [4096, 4096], P('expert', 'dp')
- grad_up: bfloat16 [32, 4096, 1024], P('expert', 'dp')
- grad_down: bfloat16 [32, 1024, 4096], P('expert', None, 'dp')
The draws below stay inside these ranges and needn't reach their ends.
Inputs may be any that keep to these rules, and one draw needn't show every extreme that they name: `expert_ids`: each row names 8 different experts. In the tokens of one device (aligned blocks of 128 rows) one expert, the same for every device, is named by exactly 64 tokens, and every other expert by at most 31 tokens; both bounds are reached on every device.
All inputs are finite; a program needn't handle non-finite values.
Results may differ from the reference program's by a relative error of at most 0.025.
Values may be sent and summed in bfloat16 or wider, within the bound.
No kernel may reach another device: no remote copies, remote signals or barrier semaphores. Data moves between devices by JAX's collectives and lax.ppermute only.
A program may use at most 64 MiB of HBM per device.

```python
import math
import jax
import jax.numpy as jnp
from jax import lax

D = 4096
FF = 1024
TOP_K = 8
TOK_DEV = 128
EXPERTS = 32
TOKENS = 4096
HOT = 64
N_DP = 8


def draw_expert_ids(key, part):
    key = jax.random.fold_in(key, 11)
    hot_expert = jax.random.randint(jax.random.fold_in(key, 1), (), 0, EXPERTS).astype(jnp.int32)
    block_count = TOKENS // TOK_DEV
    block_keys = jax.random.split(jax.random.fold_in(key, 2), block_count)

    def one_block(block_key):
        key_a, key_b, key_c = jax.random.split(block_key, 3)
        shuffle = jax.random.permutation(key_a, TOK_DEV)
        position = jnp.argsort(shuffle, stable=True)
        has_hot = (position < HOT).astype(jnp.int32)
        slot_pick = jax.random.randint(key_b, (TOK_DEV,), 0, TOP_K)
        shuffled = jax.random.permutation(key_c, EXPERTS).astype(jnp.int32)
        cold_list = shuffled[jnp.argsort((shuffled == hot_expert).astype(jnp.int32), stable=True)][:EXPERTS - 1]
        slot_ids = jnp.arange(TOP_K, dtype=jnp.int32)[None, :]
        is_hot = ((has_hot[:, None] == 1) & (slot_ids == slot_pick[:, None])).astype(jnp.int32)
        flat_hot = is_hot.reshape(TOK_DEV * TOP_K)
        cold_index = jnp.cumsum(1 - flat_hot) - (1 - flat_hot)
        cold_expert = cold_list[cold_index % (EXPERTS - 1)]
        return jnp.where(flat_hot == 1, hot_expert, cold_expert).reshape(TOK_DEV, TOP_K)
    return jax.vmap(one_block)(block_keys).reshape(TOKENS, TOP_K).astype(jnp.int32)


def shard_levels(own_key, shape, shards, smallest, high):
    def one(dim, shards_of):
        steps = jax.random.uniform(jax.random.fold_in(jax.random.fold_in(own_key, 6), dim), (shards_of,), jnp.float32, smallest / len(shards), high / len(shards))
        return jnp.repeat(jnp.exp(steps), shape[dim] // shards_of).reshape((-1,) + (1,) * (len(shape) - dim - 1))

    loudness = one(*shards[0])
    for cut in shards[1:]:
        loudness = loudness * one(*cut)
    return loudness


def bell_draw(rng, extent, scale, bound, shards=(), kind=jnp.bfloat16):
    gain = shard_levels(rng, extent, shards, -0.22, 0.18) if shards else 1.0
    result = jax.random.normal(rng, extent, jnp.float32) * scale * gain
    return jnp.minimum(jnp.maximum(result, -bound), bound).astype(kind)


def setup_inputs(seed: int = 0) -> dict:
    seeds = jax.random.split(jax.random.key(seed), 7)
    return {
        "tokens": bell_draw(seeds[0], (TOKENS, D), 1.0, 6.0, ((0, 32), (1, 8))),
        "gates": jnp.clip(jnp.exp(math.log(0.5) - 2.8134107 * jax.random.uniform(seeds[1], (TOKENS, TOP_K), jnp.float32) ** shard_levels(seeds[1], (TOKENS, TOP_K), ((0, 32),), -0.2, 0.2)), 0.03, 0.5),
        "expert_ids": draw_expert_ids(jax.random.fold_in(seeds[6], 71), 0),
        "d_mixed": bell_draw(seeds[3], (TOKENS, D), 0.5, 6.0, ((0, 32), (1, 8))),
        "w_up": bell_draw(seeds[4], (EXPERTS, D, FF), D ** -0.5, 0.09375, ((0, 32), (1, 8))),
        "w_down": bell_draw(seeds[5], (EXPERTS, FF, D), FF ** -0.5, 0.1875, ((0, 32), (2, 8))),
    }


def split_product(row_block, weight_blocks, pattern):
    partials = jnp.einsum(pattern, row_block.astype(jnp.float32), weight_blocks.astype(jnp.float32))
    partials = lax.optimization_barrier(partials.astype(jnp.bfloat16))
    return jnp.sum(partials.astype(jnp.float32), 0)


def reference(tokens, gates, expert_ids, d_mixed, w_up, w_down):
    pair_count = TOKENS * TOP_K
    part_width = D // N_DP
    routed = expert_ids.reshape(pair_count)
    onehot = (routed[:, None] == jnp.arange(EXPERTS, dtype=jnp.int32)[None, :]).astype(jnp.int32)
    counts = jnp.sum(onehot, 0)
    order_in = jnp.sum((jnp.cumsum(onehot, 0) - onehot) * onehot, 1)
    padded = (counts + 127) // 128 * 128
    offsets = jnp.cumsum(padded) - padded
    position = (offsets[routed] + order_in).astype(jnp.int32)
    blocks = (pair_count + 127) // 128 + EXPERTS
    source = jnp.full((blocks * 128,), pair_count, jnp.int32).at[position].set(jnp.arange(pair_count, dtype=jnp.int32))
    token_index = jnp.where(source < pair_count, source // TOP_K, TOKENS).astype(jnp.int32)
    zero_row = jnp.zeros((1, D), jnp.bfloat16)
    row_blocks = jnp.concatenate([tokens, zero_row], 0)[token_index].reshape(blocks, 128, D)
    scaled = (gates[:, :, None] * d_mixed[:, None, :].astype(jnp.float32)).astype(jnp.bfloat16).reshape(pair_count, D)
    scaled_blocks = jnp.concatenate([scaled, zero_row], 0)[source].reshape(blocks, 128, D)
    starts = jnp.arange(blocks, dtype=jnp.int32) * 128
    block_expert = jnp.minimum(jnp.sum((starts[:, None] >= (offsets + padded)[None, :]).astype(jnp.int32), 1), EXPERTS - 1).astype(jnp.int32)
    contract_rows = (((0,), (0,)), ((), ()))

    def block_step(totals, inputs):
        up_total, down_total = totals
        block_rows, block_scaled, expert = inputs
        up_weight = w_up[expert]
        down_weight = w_down[expert]
        pre_act = split_product(block_rows.reshape(128, N_DP, part_width), up_weight.reshape(N_DP, part_width, FF), "rjd,jdf->jrf")
        hidden = jax.nn.silu(pre_act).astype(jnp.bfloat16)
        expert_out = jnp.dot(hidden, down_weight, preferred_element_type=jnp.float32).astype(jnp.bfloat16)
        back_sum = split_product(block_scaled.reshape(128, N_DP, part_width), down_weight.reshape(FF, N_DP, part_width), "rjd,fjd->jrf")
        logistic = jax.nn.sigmoid(pre_act)
        grad_pre = (back_sum * logistic * (1.0 + pre_act * (1.0 - logistic))).astype(jnp.bfloat16)
        grad_in = lax.dot_general(grad_pre, up_weight, (((1,), (1,)), ((), ())), preferred_element_type=jnp.float32).astype(jnp.bfloat16)
        up_total = up_total.at[expert].add(lax.dot_general(block_rows, grad_pre, contract_rows, preferred_element_type=jnp.float32))
        down_total = down_total.at[expert].add(lax.dot_general(hidden, block_scaled, contract_rows, preferred_element_type=jnp.float32))
        return (up_total, down_total), (expert_out, grad_in)

    start_totals = (jnp.zeros((EXPERTS, D, FF), jnp.float32), jnp.zeros((EXPERTS, FF, D), jnp.float32))
    (up_total, down_total), (block_outs, block_ins) = lax.scan(block_step, start_totals, (row_blocks, scaled_blocks, block_expert))
    pair_out = block_outs.reshape(blocks * 128, D)[position].reshape(TOKENS, TOP_K, D)
    mixed = jnp.sum(gates[:, :, None] * pair_out.astype(jnp.float32), 1).astype(jnp.bfloat16)
    pair_in = block_ins.reshape(blocks * 128, D)[position].reshape(TOKENS, TOP_K, D)
    d_tokens = jnp.sum(pair_in.astype(jnp.float32), 1).astype(jnp.bfloat16)
    return mixed, d_tokens, up_total.astype(jnp.bfloat16), down_total.astype(jnp.bfloat16)
```

```python
import jax
import jax.numpy as jnp
from jax import lax
from jax.sharding import PartitionSpec as P

F32 = jnp.float32
BF16 = jnp.bfloat16
PLANES = [list(range(16)), list(range(16, 32))]
PARTNER = [(e, e ^ 16) for e in range(32)]
SIBLING = [(j, j ^ 1) for j in range(8)]


def ring(step):
    return [(j, ((j // 2 + step) % 4) * 2 + j % 2) for j in range(8)]


PLUS, MINUS = ring(1), ring(-1)


def mm(left, right, left_dim, right_dim):
    dims = (((left_dim,), (right_dim,)), ((), ()))
    return lax.dot_general(left, right, dims, preferred_element_type=F32)


def exchange(payload):
    return lax.all_to_all(
        payload, "expert", split_axis=0, concat_axis=0, tiled=True, axis_index_groups=PLANES
    )


def partner(block):
    return lax.ppermute(block, "expert", PARTNER)


def send(block, pairs):
    return lax.ppermute(block, "dp", pairs)


def add16(left, right):
    return (left.astype(F32) + right.astype(F32)).astype(BF16)


def after(*values):
    return lax.optimization_barrier(values)


def pick(blocks, index, axis=0):
    return lax.dynamic_index_in_dim(blocks, index, axis, keepdims=False)


def place_in_ring():
    me = lax.axis_index("dp")
    return me // 2, me % 2


def sum_over_features(rows, weight, weight_dim):
    quarter, core = place_in_ring()
    blocks = rows.reshape(4, 2, 128, -1)
    wide = weight.shape[1 - weight_dim]

    def product(which):
        part = mm(pick(blocks, which, 1).reshape(512, -1), weight, 1, weight_dim)
        return part.astype(BF16).reshape(4, 128, wide)

    came = send(product(1 - core), SIBLING)
    mine = add16(product(core), came)
    far = pick(mine, (quarter + 2) % 4)
    following = pick(mine, (quarter + 1) % 4)
    previous = pick(mine, (quarter + 3) % 4)
    here = pick(mine, quarter)
    far_top = send(far[:64], PLUS)
    far_low = send(far[64:], MINUS)
    own_low = send(following[64:], PLUS)
    own_top = send(previous[:64], MINUS)
    sum_top = send(add16(following[:64], far_top), PLUS)
    sum_low = send(add16(previous[64:], far_low), MINUS)
    top = here[:64].astype(F32) + own_top.astype(F32) + sum_top.astype(F32)
    low = here[64:].astype(F32) + own_low.astype(F32) + sum_low.astype(F32)
    return jnp.concatenate([top, low], 0)


def all_rows(share):
    quarter, core = place_in_ring()
    left = send(share, PLUS)
    right = send(share, MINUS)
    far = jnp.concatenate([send(left[:64], PLUS), send(right[64:], MINUS)], 0)
    whole = jnp.zeros((4, 2) + share.shape, share.dtype)
    for step, block in ((0, share), (1, right), (3, left), (2, far)):
        row = (quarter + step) % 4
        other = send(block, SIBLING)
        whole = lax.dynamic_update_slice(whole, block[None, None], (row, core, 0, 0))
        whole = lax.dynamic_update_slice(whole, other[None, None], (row, 1 - core, 0, 0))
    return whole.reshape(-1, share.shape[1])


def sum_small(block):
    core = lax.axis_index("dp") % 2
    half = add16(pick(block.reshape(2, 2, 32, 512), core, 1), send(
        pick(block.reshape(2, 2, 32, 512), 1 - core, 1), SIBLING))
    left = send(half, PLUS)
    right = send(half, MINUS)
    far = jnp.stack([send(left[0], PLUS), send(right[1], MINUS)], 0)
    return (
        half.astype(F32) + left.astype(F32) + right.astype(F32) + far.astype(F32)
    )


def both_cores(half):
    core = lax.axis_index("dp") % 2
    other = send(half, SIBLING)
    first = jnp.where(core == 0, half, other)
    second = jnp.where(core == 0, other, half)
    return jnp.concatenate([first, second], 1)


def per_device(tokens, gates, expert_ids, d_mixed, w_up, w_down):
    rows, width = tokens.shape
    groups, near, cap = 32, 16, 32
    up_home = w_up[0]
    down_home = w_down[0]
    me = lax.axis_index("expert")
    plane = me // near
    named = expert_ids[:, :, None] == jnp.arange(groups, dtype=jnp.int32)[None, None, :]
    names = jnp.any(named, 1)
    weight = jnp.sum(jnp.where(named, gates[:, :, None], 0.0), 1)
    earlier = jnp.arange(rows)[:, None] > jnp.arange(rows)[None, :]
    place = mm(earlier.astype(BF16), names.astype(BF16), 1, 0)
    place = jnp.where(names, place, -1.0)
    counts = jnp.sum(names.astype(jnp.int32), 0)
    hot = jnp.argmax(counts).astype(jnp.int32)
    routes = jnp.stack([place.T, weight.T], 0).reshape(2, 2, near, rows)
    mine = pick(routes, plane, 1)
    theirs = partner(pick(routes, 1 - plane, 1))
    token_pair = jnp.concatenate([tokens, partner(tokens)], 0)
    mixed_pair = jnp.concatenate([d_mixed, partner(d_mixed)], 0)

    fits = (mine[0] >= 0) & (mine[0] < cap)
    fits_theirs = (theirs[0] >= 0) & (theirs[0] < cap)
    spot = jnp.concatenate(
        [jnp.where(fits, mine[0], -1.0), jnp.where(fits_theirs, theirs[0] + cap, -1.0)], 1
    )
    spot_gate = jnp.concatenate([mine[1], theirs[1]], 1)
    hit = spot[:, None, :] == jnp.arange(2 * cap, dtype=F32)[None, :, None]
    choose = hit.astype(BF16).reshape(near * 2 * cap, 2 * rows)
    gate_map = jnp.where(hit, spot_gate[:, None, :], 0.0).reshape(near * 2 * cap, 2 * rows)
    slot_gate = jnp.sum(gate_map, 1, keepdims=True)
    hit_late = place.T[:, None, :] == jnp.arange(cap, 2 * cap, dtype=F32)[None, :, None]
    choose_late = jnp.any(hit_late, 0).astype(BF16)
    gate_late = jnp.sum(jnp.where(hit_late, weight.T[:, None, :], 0.0), 0)

    def split(block):
        return block.reshape(near, -1, width)

    def flat(block):
        return block.reshape(-1, width)

    def spread(block):
        return jnp.broadcast_to(block[None], (near,) + block.shape)

    x_send = mm(choose, token_pair, 1, 0).astype(BF16)
    x_rows = flat(exchange(split(x_send)))

    x_late = mm(choose_late, tokens, 1, 0).astype(BF16)
    s_late = (
        jnp.sum(gate_late, 1, keepdims=True) * mm(choose_late, d_mixed, 1, 0)
    ).astype(BF16)
    hot_send = jnp.concatenate(
        [spread(jnp.concatenate([x_late, s_late], 0)), split(up_home.T), split(down_home)], 1
    )
    hot_send, x_rows = after(hot_send, x_rows)
    hot_got = exchange(hot_send)

    pre = sum_over_features(x_rows, up_home, 0)
    hidden_share = (pre * jax.nn.sigmoid(pre)).astype(BF16)

    s_send = (slot_gate * mm(choose, mixed_pair, 1, 0)).astype(BF16)
    hot_got, s_send, hidden_share = after(hot_got, s_send, hidden_share)
    s_rows = flat(exchange(split(s_send)))
    hidden = all_rows(hidden_share)

    x_hot = flat(hot_got[:, :cap])
    s_hot = flat(hot_got[:, cap : 2 * cap])
    slices = pick(hot_got, hot % near)[2 * cap :]
    slices = jnp.where(hot // near == plane, slices, partner(slices))
    up_slice, down_slice = slices[:64], slices[64:]
    parts_hot = jnp.stack([mm(up_slice, x_hot, 1, 1), mm(down_slice, s_hot, 1, 1)], 0)
    sums = sum_small(parts_hot.astype(BF16))
    logistic_hot = jax.nn.sigmoid(sums[0])
    hidden_hot = sums[0] * logistic_hot
    grad_hot = sums[1] * logistic_hot * (1.0 + sums[0] * (1.0 - logistic_hot))
    hidden_hot, grad_hot = both_cores(jnp.stack([hidden_hot, grad_hot], 0).astype(BF16))
    out_hot = mm(hidden_hot, down_slice, 0, 0).astype(BF16)
    in_hot = mm(grad_hot, up_slice, 0, 0).astype(BF16)
    weight_grads = jnp.concatenate(
        [mm(hidden_hot, s_hot, 1, 0), mm(grad_hot, x_hot, 1, 0)], 0
    ).astype(BF16)
    weight_grads = add16(weight_grads, partner(weight_grads))
    hot_back = jnp.concatenate([split(out_hot), split(in_hot), spread(weight_grads)], 1)

    s_rows, hot_back = after(s_rows, hot_back)
    hot_home = exchange(hot_back)
    back = sum_over_features(s_rows, down_home, 1)
    back, pre = after(back, pre)
    logistic = jax.nn.sigmoid(pre)
    grad_share = (back * logistic * (1.0 + pre * (1.0 - logistic))).astype(BF16)

    expert_out = mm(hidden, down_home, 1, 0).astype(BF16)
    hot_home, expert_out = after(hot_home, expert_out)
    out_table = flat(exchange(split(expert_out)))
    grad_pre = all_rows(grad_share)
    out_late = jnp.sum(hot_home[:, :cap].astype(F32), 0).astype(BF16)
    in_late = jnp.sum(hot_home[:, cap : 2 * cap].astype(F32), 0).astype(BF16)
    is_hot = me == hot
    down_extra = jnp.where(is_hot, flat(hot_home[:, 2 * cap : 2 * cap + 64]), 0.0)
    up_extra = jnp.where(is_hot, flat(hot_home[:, 2 * cap + 64 :]), 0.0)

    grad_in = mm(grad_pre, up_home, 1, 1).astype(BF16)
    in_table = flat(exchange(split(grad_in)))

    def weighted(gate_block, table):
        high = gate_block.astype(BF16)
        low = (gate_block - high.astype(F32)).astype(BF16)
        return mm(high, table, 0, 0) + mm(low, table, 0, 0)

    mixed = weighted(gate_map, out_table)
    mixed = mixed[:rows] + partner(mixed[rows:].astype(BF16)).astype(F32)
    mixed = mixed + weighted(gate_late, out_late)
    d_tokens = mm(choose, in_table, 0, 0)
    d_tokens = d_tokens[:rows] + partner(d_tokens[rows:].astype(BF16)).astype(F32)
    d_tokens = d_tokens + mm(choose_late, in_late, 0, 0)
    grad_down = mm(hidden, s_rows, 0, 0) + down_extra.astype(F32)
    grad_up = mm(x_rows, grad_pre, 0, 0) + up_extra.T.astype(F32)
    return (
        mixed.astype(BF16),
        d_tokens.astype(BF16),
        grad_up.astype(BF16)[None],
        grad_down.astype(BF16)[None],
    )


def solution(mesh):
    in_specs = (
        P("expert", "dp"),
        P("expert", None),
        P("expert", None),
        P("expert", "dp"),
        P("expert", "dp", None),
        P("expert", None, "dp"),
    )
    out_specs = (
        P("expert", "dp"),
        P("expert", "dp"),
        P("expert", "dp", None),
        P("expert", None, "dp"),
    )
    return jax.shard_map(
        per_device, mesh=mesh, in_specs=in_specs, out_specs=out_specs, check_vma=False
    )
```

```python
import jax
import jax.numpy as jnp
from jax import lax
from jax.experimental import pallas as pl
from jax.experimental.pallas import tpu as pltpu
from jax.sharding import PartitionSpec as P

F32 = jnp.float32
BF16 = jnp.bfloat16
PLANES = [list(range(16)), list(range(16, 32))]
PARTNER = [(e, e ^ 16) for e in range(32)]
SIBLING = [(j, j ^ 1) for j in range(8)]


def ring(step):
    return [(j, ((j // 2 + step) % 4) * 2 + j % 2) for j in range(8)]


PLUS, MINUS = ring(1), ring(-1)


def mm(left, right, left_dim, right_dim):
    dims = (((left_dim,), (right_dim,)), ((), ()))
    return lax.dot_general(left, right, dims, preferred_element_type=F32)


def exchange(payload):
    return lax.all_to_all(payload, "expert", split_axis=0, concat_axis=0, tiled=True)


def exchange_in_plane(payload):
    return lax.all_to_all(
        payload, "expert", split_axis=0, concat_axis=0, tiled=True, axis_index_groups=PLANES
    )


def partner(block):
    return lax.ppermute(block, "expert", PARTNER)


def send(block, pairs):
    return lax.ppermute(block, "dp", pairs)


def add16(left, right):
    return (left.astype(F32) + right.astype(F32)).astype(BF16)


def after(*values):
    return lax.optimization_barrier(values)


def pick(blocks, index, axis=0):
    return lax.dynamic_index_in_dim(blocks, index, axis, keepdims=False)


def params():
    return pltpu.CompilerParams(vmem_limit_bytes=40 * 1024 * 1024)


def dispatch(spot, gate, tokens, mixed):
    groups, rows = spot.shape
    width = tokens.shape[1]
    step = 8

    def body(spot_ref, gate_ref, token_ref, mixed_ref, out_ref):
        at = lax.broadcasted_iota(jnp.int32, (step, 32, rows), 1)
        hit = at == spot_ref[...]
        scale = jnp.sum(jnp.where(hit, gate_ref[...], 0.0).reshape(step * 32, rows), 1, keepdims=True)
        one = jnp.where(hit, 1.0, 0.0).reshape(step * 32, rows).astype(BF16)
        out_ref[:, :width] = mm(one, token_ref[...], 1, 0).astype(BF16)
        out_ref[:, width:] = (scale * mm(one, mixed_ref[...], 1, 0)).astype(BF16)

    line = pl.BlockSpec((step, 1, rows), lambda e: (e, 0, 0))
    whole = pl.BlockSpec((rows, width), lambda e: (0, 0))
    return pl.pallas_call(
        body,
        grid=(groups // step,),
        in_specs=[line, line, whole, whole],
        out_specs=pl.BlockSpec((32 * step, 2 * width), lambda e: (e, 0)),
        out_shape=jax.ShapeDtypeStruct((32 * groups, 2 * width), BF16),
        compiler_params=params(),
    )(spot[:, None], gate[:, None], tokens, mixed)


ORDER = ((0, 2), (1, 1), (1, 2), (0, 3), (0, 1), (1, 3), (0, 0), (1, 0))


def parts_for_sibling(rows, up, down):
    def body(row_ref, up_ref, down_ref, out_ref):
        product = (
            mm(row_ref[:, :512], up_ref[...], 1, 0).astype(BF16),
            mm(row_ref[:, 512:], down_ref[...], 1, 1).astype(BF16),
        )
        for i, (which, block) in enumerate(ORDER):
            out_ref[i] = product[which][128 * block : 128 * block + 128]

    return pl.pallas_call(
        body,
        out_shape=jax.ShapeDtypeStruct((8, 128, 1024), BF16),
        compiler_params=params(),
    )(rows, up, down)


def parts_with_sibling(rows, up, down, came):
    def body(row_ref, up_ref, down_ref, came_ref, *out_refs):
        product = (
            mm(row_ref[:, :512], up_ref[...], 1, 0),
            mm(row_ref[:, 512:], down_ref[...], 1, 1),
        )
        for i, (which, block) in enumerate(ORDER):
            part = product[which][128 * block : 128 * block + 128]
            out_refs[i // 2][i % 2] = (part + came_ref[i].astype(F32)).astype(BF16)

    return pl.pallas_call(
        body,
        out_shape=[jax.ShapeDtypeStruct((2, 128, 1024), BF16)] * 4,
        compiler_params=params(),
    )(rows, up, down, came)


def sum_over_features(own, other, up, down):
    came = send(parts_for_sibling(other, up, down), SIBLING)
    first_up, first_down, second, here = parts_with_sibling(own, up, down, came)
    got_up, got_down = after(send(first_up, PLUS), send(first_down, MINUS))
    next_up, next_down, got_up, got_down, here = after(
        add16(second[0], got_up[0]), add16(second[1], got_down[0]), got_up, got_down, here
    )
    up_second = send(next_up, PLUS)
    down_second = send(next_down, MINUS)
    pre = here[0].astype(F32) + got_down[1].astype(F32) + up_second.astype(F32)
    back = here[1].astype(F32) + got_up[1].astype(F32) + down_second.astype(F32)
    return pre, back


def finish(pairs, down, up):
    count = pairs.shape[0]

    def body(pair_ref, down_ref, up_ref, out_ref):
        out_ref[:, :512] = mm(pair_ref[0, 0], down_ref[...], 1, 0).astype(BF16)
        out_ref[:, 512:] = mm(pair_ref[0, 1], up_ref[...], 1, 1).astype(BF16)

    return pl.pallas_call(
        body,
        grid=(count,),
        in_specs=[
            pl.BlockSpec((1, 2, 128, 1024), lambda i: (i, 0, 0, 0)),
            pl.BlockSpec(down.shape, lambda i: (0, 0)),
            pl.BlockSpec(up.shape, lambda i: (0, 0)),
        ],
        out_specs=pl.BlockSpec((128, 1024), lambda i: (i, 0)),
        out_shape=jax.ShapeDtypeStruct((128 * count, 1024), BF16),
        compiler_params=params(),
    )(pairs, down, up)


def all_blocks(share):
    left = send(share, PLUS)
    right = send(share, MINUS)
    left, right = after(left, right)
    left_hidden, right_grad, left, right = after(left[0], right[1], left, right)
    far_hidden = send(left_hidden, PLUS)
    far_grad = send(right_grad, MINUS)
    near = jnp.stack([share, right, left], 0)
    far = jnp.stack([far_hidden, far_grad], 0)[None]
    return near, far, send(near, SIBLING), send(far, SIBLING)


def ordered(near, far):
    return jnp.concatenate([near[:2], far, near[2:]], 0)


def sum_small(block):
    core = lax.axis_index("dp") % 2
    halves = block.reshape(2, 2, 32, 512)
    half = add16(pick(halves, core, 1), send(pick(halves, 1 - core, 1), SIBLING))
    total = half.astype(F32)
    for step in (1, 2, 3):
        total = total + send(half, ring(step)).astype(F32)
    return total


def both_cores(half):
    core = lax.axis_index("dp") % 2
    other = send(half, SIBLING)
    first = jnp.where(core == 0, half, other)
    second = jnp.where(core == 0, other, half)
    return jnp.concatenate([first, second], 1)


def two_parts(block):
    high = block.astype(BF16)
    return high, (block - high.astype(F32)).astype(BF16)


def per_device(tokens, gates, expert_ids, d_mixed, w_up, w_down):
    rows, width = tokens.shape
    groups, near, cap = 32, 16, 32
    up_home = w_up[0]
    down_home = w_down[0]
    me = lax.axis_index("expert")
    at = lax.axis_index("dp")
    quarter, core = at // 2, at % 2
    plane = me // near

    def split(block):
        return block.reshape(near, -1, block.shape[-1])

    def flat(block):
        return block.reshape(-1, block.shape[-1])

    def spread(block):
        return jnp.broadcast_to(block[None], (near,) + block.shape)

    named = expert_ids[:, :, None] == jnp.arange(groups, dtype=jnp.int32)[None, None, :]
    names = jnp.any(named, 1)
    weight = jnp.sum(jnp.where(named, gates[:, :, None], 0.0), 1)
    earlier = jnp.arange(rows)[:, None] > jnp.arange(rows)[None, :]
    place = mm(earlier.astype(BF16), names.astype(BF16), 1, 0).astype(jnp.int32)
    place = jnp.where(names, place, -1)
    hot = jnp.argmax(jnp.sum(names.astype(jnp.int32), 0)).astype(jnp.int32)
    spot = (((place >> 3) - quarter) & 3) * 8 + (place & 7)
    spot = jnp.where((place >= 0) & (place < cap), spot, -1)
    to_send = dispatch(spot.T, weight.T, tokens, d_mixed)
    received = exchange(to_send.reshape(groups, cap, 2 * width))

    hit = spot[:, :, None] == jnp.arange(cap, dtype=jnp.int32)[None, None, :]
    gate_map = jnp.where(hit, weight[:, :, None], 0.0).reshape(rows, groups * cap)
    collect = jnp.concatenate(
        [*two_parts(gate_map), hit.astype(BF16).reshape(rows, groups * cap)], 0
    )
    hit_late = place.T[:, None, :] == jnp.arange(cap, 2 * cap, dtype=jnp.int32)[None, :, None]
    choose_late = jnp.any(hit_late, 0).astype(BF16)
    gate_late = jnp.sum(jnp.where(hit_late, weight.T[:, None, :], 0.0), 0)

    x_late = mm(choose_late, tokens, 1, 0).astype(BF16)
    s_late = mm(choose_late, d_mixed, 1, 0) * jnp.sum(gate_late, 1, keepdims=True)
    hot_send = jnp.concatenate(
        [
            spread(jnp.concatenate([x_late, s_late.astype(BF16)], 0)),
            split(up_home.T),
            split(down_home),
        ],
        1,
    )
    hot_send, received, collect = after(hot_send, received, collect)
    hot_got = exchange_in_plane(hot_send)

    received = received.reshape(2, near, 4, 8, 2 * width)

    def by_quarter(which):
        return pick(received, which).transpose(1, 0, 2, 3).reshape(512, 2 * width)

    own_rows, other_rows = by_quarter(core), by_quarter(1 - core)
    pre, back = sum_over_features(own_rows, other_rows, up_home, down_home)
    hot_got, pre, back = after(hot_got, pre, back)
    logistic = jax.nn.sigmoid(pre)
    share = jnp.stack(
        [pre * logistic, back * logistic * (1.0 + pre * (1.0 - logistic))], 0
    ).astype(BF16)

    x_hot = flat(hot_got[:, :cap])
    s_hot = flat(hot_got[:, cap : 2 * cap])
    slices = pick(hot_got, hot % near)[2 * cap :]
    slices = jnp.where(hot // near == plane, slices, partner(slices))
    up_slice, down_slice = slices[:64], slices[64:]
    parts_hot = jnp.stack([mm(up_slice, x_hot, 1, 1), mm(down_slice, s_hot, 1, 1)], 0)
    sums_hot = sum_small(parts_hot.astype(BF16))
    logistic_hot = jax.nn.sigmoid(sums_hot[0])
    hidden_hot = sums_hot[0] * logistic_hot
    grad_hot = sums_hot[1] * logistic_hot * (1.0 + sums_hot[0] * (1.0 - logistic_hot))
    hidden_hot, grad_hot = both_cores(jnp.stack([hidden_hot, grad_hot], 0).astype(BF16))
    out_hot = mm(hidden_hot, down_slice, 0, 0).astype(BF16)
    in_hot = mm(grad_hot, up_slice, 0, 0).astype(BF16)
    weight_grads = jnp.concatenate(
        [mm(hidden_hot, s_hot, 1, 0), mm(grad_hot, x_hot, 1, 0)], 0
    ).astype(BF16)
    weight_grads = add16(weight_grads, partner(weight_grads))
    share, weight_grads = after(share, weight_grads)
    hot_back = jnp.concatenate([split(out_hot), split(in_hot), spread(weight_grads)], 1)
    hot_home = exchange_in_plane(hot_back)

    pieces = all_blocks(share)
    own_near, own_far, other_near, other_far = [finish(p, down_home, up_home) for p in pieces]

    def by_source(near_rows, far_rows):
        rows_out = jnp.concatenate([near_rows[:256], far_rows, near_rows[256:]], 0)
        return rows_out.reshape(4, near, 8, 2 * width).transpose(1, 0, 2, 3)

    own_out, other_out = by_source(own_near, own_far), by_source(other_near, other_far)
    out_rows = jnp.stack(
        [jnp.where(core == 0, own_out, other_out), jnp.where(core == 0, other_out, own_out)], 0
    )
    out_rows, hot_home, *pieces = after(out_rows, hot_home, *pieces)
    table = flat(exchange(out_rows.reshape(groups, cap, 2 * width)))

    out_late = jnp.sum(hot_home[:, :cap].astype(F32), 0).astype(BF16)
    in_late = jnp.sum(hot_home[:, cap : 2 * cap].astype(F32), 0).astype(BF16)
    is_hot = me == hot
    down_extra = jnp.where(is_hot, flat(hot_home[:, 2 * cap : 2 * cap + 64]), 0)
    up_extra = jnp.where(is_hot, flat(hot_home[:, 2 * cap + 64 :]), 0).T
    units = jnp.concatenate([ordered(pieces[0], pieces[1]), ordered(pieces[2], pieces[3])], 0)
    hidden, grad_pre = units[:, 0].reshape(1024, 1024), units[:, 1].reshape(1024, 1024)
    rows_in = jnp.concatenate([own_rows, other_rows], 0)
    grad_up = mm(rows_in[:, :width], grad_pre, 0, 0) + up_extra.astype(F32)
    grad_down = mm(hidden, rows_in[:, width:], 0, 0) + down_extra.astype(F32)
    high_late, low_late = two_parts(gate_late)
    mixed_late = mm(high_late, out_late, 0, 0) + mm(low_late, out_late, 0, 0)
    tokens_late = mm(choose_late, in_late, 0, 0)

    total = mm(collect, table, 1, 0)
    mixed = total[:rows, :width] + total[rows : 2 * rows, :width] + mixed_late
    d_tokens = total[2 * rows :, width:] + tokens_late
    return (
        mixed.astype(BF16),
        d_tokens.astype(BF16),
        grad_up.astype(BF16)[None],
        grad_down.astype(BF16)[None],
    )


def solution(mesh):
    in_specs = (
        P("expert", "dp"),
        P("expert", None),
        P("expert", None),
        P("expert", "dp"),
        P("expert", "dp", None),
        P("expert", None, "dp"),
    )
    out_specs = (
        P("expert", "dp"),
        P("expert", "dp"),
        P("expert", "dp", None),
        P("expert", None, "dp"),
    )
    return jax.shard_map(
        per_device, mesh=mesh, in_specs=in_specs, out_specs=out_specs, check_vma=False
    )
```

```python
import jax
import jax.numpy as jnp
from jax import lax
from jax.experimental import pallas as pl
from jax.experimental.pallas import tpu as pltpu
from jax.sharding import PartitionSpec as P

F32 = jnp.float32
BF16 = jnp.bfloat16
PLANES = [list(range(16)), list(range(16, 32))]
PARTNER = [(e, e ^ 16) for e in range(32)]
SIBLING = [(j, j ^ 1) for j in range(8)]


def ring(step):
    return [(j, ((j // 2 + step) % 4) * 2 + j % 2) for j in range(8)]


PLUS, MINUS = ring(1), ring(-1)


def mm(left, right, left_dim, right_dim):
    dims = (((left_dim,), (right_dim,)), ((), ()))
    return lax.dot_general(left, right, dims, preferred_element_type=F32)


def exchange(payload):
    return lax.all_to_all(payload, "expert", split_axis=0, concat_axis=0, tiled=True)


def exchange_in_plane(payload):
    return lax.all_to_all(
        payload, "expert", split_axis=0, concat_axis=0, tiled=True, axis_index_groups=PLANES
    )


def partner(block):
    return lax.ppermute(block, "expert", PARTNER)


def send(block, pairs):
    return lax.ppermute(block, "dp", pairs)


def add16(left, right):
    return (left.astype(F32) + right.astype(F32)).astype(BF16)


def after(*values):
    return lax.optimization_barrier(values)


def pick(blocks, index, axis=0):
    return lax.dynamic_index_in_dim(blocks, index, axis, keepdims=False)


def params():
    return pltpu.CompilerParams(vmem_limit_bytes=40 * 1024 * 1024)


def dispatch(spot, gate, tokens, mixed):
    groups, rows = spot.shape
    width = tokens.shape[1]
    step = 8

    def body(spot_ref, gate_ref, token_ref, mixed_ref, out_ref):
        at = lax.broadcasted_iota(jnp.int32, (step, 32, rows), 1)
        hit = at == spot_ref[...]
        scale = jnp.sum(jnp.where(hit, gate_ref[...], 0.0).reshape(step * 32, rows), 1, keepdims=True)
        one = jnp.where(hit, 1.0, 0.0).reshape(step * 32, rows).astype(BF16)
        out_ref[:, :width] = mm(one, token_ref[...], 1, 0).astype(BF16)
        out_ref[:, width:] = (scale * mm(one, mixed_ref[...], 1, 0)).astype(BF16)

    line = pl.BlockSpec((step, 1, rows), lambda e: (e, 0, 0))
    whole = pl.BlockSpec((rows, width), lambda e: (0, 0))
    return pl.pallas_call(
        body,
        grid=(groups // step,),
        in_specs=[line, line, whole, whole],
        out_specs=pl.BlockSpec((32 * step, 2 * width), lambda e: (e, 0)),
        out_shape=jax.ShapeDtypeStruct((32 * groups, 2 * width), BF16),
        compiler_params=params(),
    )(spot[:, None], gate[:, None], tokens, mixed)


ORDER = ((0, 2), (1, 2), (1, 1), (0, 3), (0, 1), (1, 3), (0, 0), (1, 0))


def parts_for_sibling(rows, up, down):
    def body(row_ref, up_ref, down_ref, out_ref):
        product = (
            mm(row_ref[:, :512], up_ref[...], 1, 0).astype(BF16),
            mm(row_ref[:, 512:], down_ref[...], 1, 1).astype(BF16),
        )
        for i, (which, block) in enumerate(ORDER):
            out_ref[i] = product[which][128 * block : 128 * block + 128]

    return pl.pallas_call(
        body,
        out_shape=jax.ShapeDtypeStruct((8, 128, 1024), BF16),
        compiler_params=params(),
    )(rows, up, down)


def parts_with_sibling(rows, up, down, came):
    def body(row_ref, up_ref, down_ref, came_ref, *out_refs):
        product = (
            mm(row_ref[:, :512], up_ref[...], 1, 0),
            mm(row_ref[:, 512:], down_ref[...], 1, 1),
        )
        for i, (which, block) in enumerate(ORDER):
            part = product[which][128 * block : 128 * block + 128]
            out_refs[i][...] = (part + came_ref[i].astype(F32)).astype(BF16)

    return pl.pallas_call(
        body,
        out_shape=[jax.ShapeDtypeStruct((128, 1024), BF16)] * 8,
        compiler_params=params(),
    )(rows, up, down, came)


def sum_over_features(own, other, up, down):
    came = send(parts_for_sibling(other, up, down), SIBLING)
    parts = parts_with_sibling(own, up, down, came)
    far_up, far_down, near_back, near_pre, next_up, next_down, here_pre, here_back = parts
    got_up, got_down = after(send(far_up, PLUS), send(far_down, MINUS))
    near_back, near_pre = send(near_back, PLUS), send(near_pre, MINUS)
    next_up, next_down = after(add16(next_up, got_up), add16(next_down, got_down))
    up_second = send(next_up, PLUS)
    down_second = send(next_down, MINUS)
    pre = here_pre.astype(F32) + near_pre.astype(F32) + up_second.astype(F32)
    back = here_back.astype(F32) + near_back.astype(F32) + down_second.astype(F32)
    return pre, back, next_up, next_down


def finish(pairs, down, up):
    count = pairs.shape[0]

    def body(pair_ref, down_ref, up_ref, out_ref):
        out_ref[:, :512] = mm(pair_ref[0, 0], down_ref[...], 1, 0).astype(BF16)
        out_ref[:, 512:] = mm(pair_ref[0, 1], up_ref[...], 1, 1).astype(BF16)

    return pl.pallas_call(
        body,
        grid=(count,),
        in_specs=[
            pl.BlockSpec((1, 2, 128, 1024), lambda i: (i, 0, 0, 0)),
            pl.BlockSpec(down.shape, lambda i: (0, 0)),
            pl.BlockSpec(up.shape, lambda i: (0, 0)),
        ],
        out_specs=pl.BlockSpec((128, 1024), lambda i: (i, 0)),
        out_shape=jax.ShapeDtypeStruct((128 * count, 1024), BF16),
        compiler_params=params(),
    )(pairs, down, up)


def all_blocks(share, hot_back, use):
    left = send(share, PLUS)
    right = send(share, MINUS)
    other_share = send(share, SIBLING)
    hot_back, other_share = after(hot_back, other_share)
    left, right = after(left, right)
    left_hidden, right_grad, left, right = after(left[0], right[1], left, right)
    far_hidden = send(left_hidden, PLUS)
    far_grad = send(right_grad, MINUS)
    sides = jnp.stack([right, left], 0)
    other_sides = send(sides, SIBLING)
    near = jnp.concatenate([share[None], sides], 0)
    other_near = jnp.concatenate([other_share[None], other_sides], 0)
    used_near, used_other = use(near), use(other_near)
    far_hidden, far_grad, used_near, used_other = after(far_hidden, far_grad, used_near, used_other)
    far = jnp.stack([far_hidden, far_grad], 0)[None]
    other_far = send(far, SIBLING)
    used = used_near, use(far), used_other, use(other_far)
    return (near, far, other_near, other_far), used, hot_back


def ordered(near, far):
    return jnp.concatenate([near[:2], far, near[2:]], 0)


def sum_small(block, *earlier):
    core = lax.axis_index("dp") % 2
    halves = block.reshape(2, 2, 32, 512)
    half = add16(pick(halves, core, 1), send(pick(halves, 1 - core, 1), SIBLING))
    half = after(half, *earlier)[0]
    total = half.astype(F32)
    for step in (1, 2, 3):
        total = total + send(half, ring(step)).astype(F32)
    return total


def both_cores(half):
    core = lax.axis_index("dp") % 2
    other = send(half, SIBLING)
    first = jnp.where(core == 0, half, other)
    second = jnp.where(core == 0, other, half)
    return jnp.concatenate([first, second], 1)


def two_parts(block):
    high = block.astype(BF16)
    return high, (block - high.astype(F32)).astype(BF16)


def per_device(tokens, gates, expert_ids, d_mixed, w_up, w_down):
    rows, width = tokens.shape
    groups, near, cap = 32, 16, 32
    up_home = w_up[0]
    down_home = w_down[0]
    me = lax.axis_index("expert")
    at = lax.axis_index("dp")
    quarter, core = at // 2, at % 2
    plane = me // near

    def split(block):
        return block.reshape(near, -1, block.shape[-1])

    def flat(block):
        return block.reshape(-1, block.shape[-1])

    def spread(block):
        return jnp.broadcast_to(block[None], (near,) + block.shape)

    named = expert_ids[:, :, None] == jnp.arange(groups, dtype=jnp.int32)[None, None, :]
    names = jnp.any(named, 1)
    weight = jnp.sum(jnp.where(named, gates[:, :, None], 0.0), 1)
    earlier = jnp.arange(rows)[:, None] > jnp.arange(rows)[None, :]
    place = mm(earlier.astype(BF16), names.astype(BF16), 1, 0).astype(jnp.int32)
    place = jnp.where(names, place, -1)
    hot = jnp.argmax(jnp.sum(names.astype(jnp.int32), 0)).astype(jnp.int32)
    spot = (((place >> 3) - quarter) & 3) * 8 + (place & 7)
    spot = jnp.where((place >= 0) & (place < cap), spot, -1)
    to_send = dispatch(spot.T, weight.T, tokens, d_mixed)
    received = exchange(to_send.reshape(groups, cap, 2 * width))

    hit = spot[:, :, None] == jnp.arange(cap, dtype=jnp.int32)[None, None, :]
    gate_map = jnp.where(hit, weight[:, :, None], 0.0).reshape(rows, groups * cap)
    collect = jnp.concatenate(
        [*two_parts(gate_map), hit.astype(BF16).reshape(rows, groups * cap)], 0
    )
    hit_late = place.T[:, None, :] == jnp.arange(cap, 2 * cap, dtype=jnp.int32)[None, :, None]
    choose_late = jnp.any(hit_late, 0).astype(BF16)
    gate_late = jnp.sum(jnp.where(hit_late, weight.T[:, None, :], 0.0), 0)

    x_late = mm(choose_late, tokens, 1, 0).astype(BF16)
    s_late = mm(choose_late, d_mixed, 1, 0) * jnp.sum(gate_late, 1, keepdims=True)
    hot_send = jnp.concatenate(
        [
            spread(jnp.concatenate([x_late, s_late.astype(BF16)], 0)),
            split(up_home.T),
            split(down_home),
        ],
        1,
    )
    hot_send, received, collect = after(hot_send, received, collect)
    hot_got = exchange_in_plane(hot_send)

    received = received.reshape(2, near, 4, 8, 2 * width)

    def by_quarter(which):
        return pick(received, which).transpose(1, 0, 2, 3).reshape(512, 2 * width)

    own_rows, other_rows = by_quarter(core), by_quarter(1 - core)
    pre, back, *started = sum_over_features(own_rows, other_rows, up_home, down_home)
    hot_got = after(hot_got, *started)[0]
    logistic = jax.nn.sigmoid(pre)
    share = jnp.stack(
        [pre * logistic, back * logistic * (1.0 + pre * (1.0 - logistic))], 0
    ).astype(BF16)

    x_hot = flat(hot_got[:, :cap])
    s_hot = flat(hot_got[:, cap : 2 * cap])
    slices = pick(hot_got, hot % near)[2 * cap :]
    slices = jnp.where(hot // near == plane, slices, partner(slices))
    up_slice, down_slice = slices[:64], slices[64:]
    parts_hot = jnp.stack([mm(up_slice, x_hot, 1, 1), mm(down_slice, s_hot, 1, 1)], 0)
    sums_hot = sum_small(parts_hot.astype(BF16), pre, back)
    logistic_hot = jax.nn.sigmoid(sums_hot[0])
    hidden_hot = sums_hot[0] * logistic_hot
    grad_hot = sums_hot[1] * logistic_hot * (1.0 + sums_hot[0] * (1.0 - logistic_hot))
    hidden_hot, grad_hot = both_cores(jnp.stack([hidden_hot, grad_hot], 0).astype(BF16))
    out_hot = mm(hidden_hot, down_slice, 0, 0).astype(BF16)
    in_hot = mm(grad_hot, up_slice, 0, 0).astype(BF16)
    weight_grads = jnp.concatenate(
        [mm(hidden_hot, s_hot, 1, 0), mm(grad_hot, x_hot, 1, 0)], 0
    ).astype(BF16)
    weight_grads = add16(weight_grads, partner(weight_grads))
    share, weight_grads = after(share, weight_grads)
    hot_back = jnp.concatenate([split(out_hot), split(in_hot), spread(weight_grads)], 1)
    pieces, used, hot_back = all_blocks(
        share, hot_back, lambda pairs: finish(pairs, down_home, up_home)
    )
    hot_home = exchange_in_plane(hot_back)
    own_near, own_far, other_near, other_far = used

    def by_source(near_rows, far_rows):
        rows_out = jnp.concatenate([near_rows[:256], far_rows, near_rows[256:]], 0)
        return rows_out.reshape(4, near, 8, 2 * width).transpose(1, 0, 2, 3)

    own_out, other_out = by_source(own_near, own_far), by_source(other_near, other_far)
    out_rows = jnp.stack(
        [jnp.where(core == 0, own_out, other_out), jnp.where(core == 0, other_out, own_out)], 0
    )
    out_rows, hot_home, *pieces = after(out_rows, hot_home, *pieces)
    table = flat(exchange(out_rows.reshape(groups, cap, 2 * width)))

    out_late = jnp.sum(hot_home[:, :cap].astype(F32), 0).astype(BF16)
    in_late = jnp.sum(hot_home[:, cap : 2 * cap].astype(F32), 0).astype(BF16)
    is_hot = me == hot
    down_extra = jnp.where(is_hot, flat(hot_home[:, 2 * cap : 2 * cap + 64]), 0)
    up_extra = jnp.where(is_hot, flat(hot_home[:, 2 * cap + 64 :]), 0).T
    units = jnp.concatenate([ordered(pieces[0], pieces[1]), ordered(pieces[2], pieces[3])], 0)
    hidden, grad_pre = units[:, 0].reshape(1024, 1024), units[:, 1].reshape(1024, 1024)
    rows_in = jnp.concatenate([own_rows, other_rows], 0)
    grad_up = mm(rows_in[:, :width], grad_pre, 0, 0) + up_extra.astype(F32)
    grad_down = mm(hidden, rows_in[:, width:], 0, 0) + down_extra.astype(F32)
    high_late, low_late = two_parts(gate_late)
    mixed_late = mm(high_late, out_late, 0, 0) + mm(low_late, out_late, 0, 0)
    tokens_late = mm(choose_late, in_late, 0, 0)

    total = mm(collect, table, 1, 0)
    mixed = total[:rows, :width] + total[rows : 2 * rows, :width] + mixed_late
    d_tokens = total[2 * rows :, width:] + tokens_late
    return (
        mixed.astype(BF16),
        d_tokens.astype(BF16),
        grad_up.astype(BF16)[None],
        grad_down.astype(BF16)[None],
    )


def solution(mesh):
    in_specs = (
        P("expert", "dp"),
        P("expert", None),
        P("expert", None),
        P("expert", "dp"),
        P("expert", "dp", None),
        P("expert", None, "dp"),
    )
    out_specs = (
        P("expert", "dp"),
        P("expert", "dp"),
        P("expert", "dp", None),
        P("expert", None, "dp"),
    )
    return jax.shard_map(
        per_device, mesh=mesh, in_specs=in_specs, out_specs=out_specs, check_vma=False
    )
```

```python
import jax
import jax.numpy as jnp
from jax import lax
from jax.experimental import pallas as pl
from jax.experimental.pallas import tpu as pltpu
from jax.sharding import PartitionSpec as P

F32 = jnp.float32
BF16 = jnp.bfloat16
PLANES = [list(range(16)), list(range(16, 32))]
PARTNER = [(e, e ^ 16) for e in range(32)]
SIBLING = [(j, j ^ 1) for j in range(8)]


def ring(step):
    return [(j, ((j // 2 + step) % 4) * 2 + j % 2) for j in range(8)]


PLUS, MINUS = ring(1), ring(-1)


def mm(left, right, left_dim, right_dim):
    dims = (((left_dim,), (right_dim,)), ((), ()))
    return lax.dot_general(left, right, dims, preferred_element_type=F32)


def exchange(payload):
    return lax.all_to_all(payload, "expert", split_axis=0, concat_axis=0, tiled=True)


def exchange_in_plane(payload):
    return lax.all_to_all(
        payload, "expert", split_axis=0, concat_axis=0, tiled=True, axis_index_groups=PLANES
    )


def partner(block):
    return lax.ppermute(block, "expert", PARTNER)


def send(block, pairs):
    return lax.ppermute(block, "dp", pairs)


def add16(left, right):
    return (left.astype(F32) + right.astype(F32)).astype(BF16)


def after(*values):
    return lax.optimization_barrier(values)


def pick(blocks, index, axis=0):
    return lax.dynamic_index_in_dim(blocks, index, axis, keepdims=False)


def params():
    return pltpu.CompilerParams(vmem_limit_bytes=40 * 1024 * 1024)


def dispatch(spot, gate, tokens, mixed):
    groups, rows = spot.shape
    width = tokens.shape[1]
    step = 8

    def body(spot_ref, gate_ref, token_ref, mixed_ref, out_ref):
        at = lax.broadcasted_iota(jnp.int32, (step, 32, rows), 1)
        hit = at == spot_ref[...]
        scale = jnp.sum(jnp.where(hit, gate_ref[...], 0.0).reshape(step * 32, rows), 1, keepdims=True)
        one = jnp.where(hit, 1.0, 0.0).reshape(step * 32, rows).astype(BF16)
        out_ref[:, :width] = mm(one, token_ref[...], 1, 0).astype(BF16)
        out_ref[:, width:] = (scale * mm(one, mixed_ref[...], 1, 0)).astype(BF16)

    line = pl.BlockSpec((step, 1, rows), lambda e: (e, 0, 0))
    whole = pl.BlockSpec((rows, width), lambda e: (0, 0))
    return pl.pallas_call(
        body,
        grid=(groups // step,),
        in_specs=[line, line, whole, whole],
        out_specs=pl.BlockSpec((32 * step, 2 * width), lambda e: (e, 0)),
        out_shape=jax.ShapeDtypeStruct((32 * groups, 2 * width), BF16),
        compiler_params=params(),
    )(spot[:, None], gate[:, None], tokens, mixed)


ORDER = ((0, 2), (1, 2), (1, 1), (0, 3), (0, 1), (1, 3), (0, 0), (1, 0))


def parts_for_sibling(rows, up, down):
    def body(row_ref, up_ref, down_ref, out_ref):
        product = (
            mm(row_ref[:, :512], up_ref[...], 1, 0).astype(BF16),
            mm(row_ref[:, 512:], down_ref[...], 1, 1).astype(BF16),
        )
        for i, (which, block) in enumerate(ORDER):
            out_ref[i] = product[which][128 * block : 128 * block + 128]

    return pl.pallas_call(
        body,
        out_shape=jax.ShapeDtypeStruct((8, 128, 1024), BF16),
        compiler_params=params(),
    )(rows, up, down)


def parts_with_sibling(rows, up, down, came):
    def body(row_ref, up_ref, down_ref, came_ref, *out_refs):
        product = (
            mm(row_ref[:, :512], up_ref[...], 1, 0),
            mm(row_ref[:, 512:], down_ref[...], 1, 1),
        )
        for i, (which, block) in enumerate(ORDER):
            part = product[which][128 * block : 128 * block + 128]
            out_refs[i][...] = (part + came_ref[i].astype(F32)).astype(BF16)

    return pl.pallas_call(
        body,
        out_shape=[jax.ShapeDtypeStruct((128, 1024), BF16)] * 8,
        compiler_params=params(),
    )(rows, up, down, came)


def sum_over_features(own, other, up, down):
    came = send(parts_for_sibling(other, up, down), SIBLING)
    parts = parts_with_sibling(own, up, down, came)
    far_up, far_down, near_back, near_pre, next_up, next_down, here_pre, here_back = parts
    got_up, got_down = after(send(far_up, PLUS), send(far_down, MINUS))
    near_back, near_pre = send(near_back, PLUS), send(near_pre, MINUS)
    next_up, next_down = after(add16(next_up, got_up), add16(next_down, got_down))
    up_second = send(next_up, PLUS)
    down_second = send(next_down, MINUS)
    pre = here_pre.astype(F32) + near_pre.astype(F32) + up_second.astype(F32)
    back = here_back.astype(F32) + near_back.astype(F32) + down_second.astype(F32)
    return pre, back, next_up, next_down


def finish(pairs, down, up):
    count = pairs.shape[0]

    def body(pair_ref, down_ref, up_ref, out_ref):
        out_ref[:, :512] = mm(pair_ref[0, 0], down_ref[...], 1, 0).astype(BF16)
        out_ref[:, 512:] = mm(pair_ref[0, 1], up_ref[...], 1, 1).astype(BF16)

    return pl.pallas_call(
        body,
        grid=(count,),
        in_specs=[
            pl.BlockSpec((1, 2, 128, 1024), lambda i: (i, 0, 0, 0)),
            pl.BlockSpec(down.shape, lambda i: (0, 0)),
            pl.BlockSpec(up.shape, lambda i: (0, 0)),
        ],
        out_specs=pl.BlockSpec((128, 1024), lambda i: (i, 0)),
        out_shape=jax.ShapeDtypeStruct((128 * count, 1024), BF16),
        compiler_params=params(),
    )(pairs, down, up)


def all_blocks(share, hot_back, use):
    left = send(share, PLUS)
    right = send(share, MINUS)
    other_share = send(share, SIBLING)
    hot_back, other_share = after(hot_back, other_share)
    left, right = after(left, right)
    left_hidden, right_grad, left, right = after(left[0], right[1], left, right)
    far_hidden = send(left_hidden, PLUS)
    far_grad = send(right_grad, MINUS)
    sides = jnp.stack([right, left], 0)
    other_sides = send(sides, SIBLING)
    near = jnp.concatenate([share[None], sides], 0)
    other_near = jnp.concatenate([other_share[None], other_sides], 0)
    used_near, used_other = use(near), use(other_near)
    far_hidden, far_grad, used_near, used_other = after(far_hidden, far_grad, used_near, used_other)
    far = jnp.stack([far_hidden, far_grad], 0)[None]
    other_far = send(far, SIBLING)
    used = used_near, use(far), used_other, use(other_far)
    return (near, far, other_near, other_far), used, hot_back


def ordered(near, far):
    return jnp.concatenate([near[:2], far, near[2:]], 0)


def sum_small(block, *earlier):
    core = lax.axis_index("dp") % 2
    halves = block.reshape(2, 2, 32, 512)
    half = add16(pick(halves, core, 1), send(pick(halves, 1 - core, 1), SIBLING))
    half = after(half, *earlier)[0]
    total = half.astype(F32)
    for step in (1, 2, 3):
        total = total + send(half, ring(step)).astype(F32)
    return total


def both_cores(half):
    core = lax.axis_index("dp") % 2
    other = send(half, SIBLING)
    first = jnp.where(core == 0, half, other)
    second = jnp.where(core == 0, other, half)
    return jnp.concatenate([first, second], 1)


def combine(collect, table, mixed_late, tokens_late):
    def body(collect_ref, table_ref, mixed_late_ref, tokens_late_ref, mixed_ref, tokens_ref):
        mixed = mm(collect_ref[:256], table_ref[:, :512], 1, 0)
        mixed_ref[...] = (mixed[:128] + mixed[128:] + mixed_late_ref[...]).astype(BF16)
        back = mm(collect_ref[256:], table_ref[:, 512:], 1, 0)
        tokens_ref[...] = (back + tokens_late_ref[...]).astype(BF16)

    return pl.pallas_call(
        body,
        out_shape=[jax.ShapeDtypeStruct((128, 512), BF16)] * 2,
        compiler_params=params(),
    )(collect, table, mixed_late, tokens_late)


def two_parts(block):
    high = block.astype(BF16)
    return high, (block - high.astype(F32)).astype(BF16)


def per_device(tokens, gates, expert_ids, d_mixed, w_up, w_down):
    rows, width = tokens.shape
    groups, near, cap = 32, 16, 32
    up_home = w_up[0]
    down_home = w_down[0]
    me = lax.axis_index("expert")
    at = lax.axis_index("dp")
    quarter, core = at // 2, at % 2
    plane = me // near

    def split(block):
        return block.reshape(near, -1, block.shape[-1])

    def flat(block):
        return block.reshape(-1, block.shape[-1])

    def spread(block):
        return jnp.broadcast_to(block[None], (near,) + block.shape)

    named = expert_ids[:, :, None] == jnp.arange(groups, dtype=jnp.int32)[None, None, :]
    names = jnp.any(named, 1)
    weight = jnp.sum(jnp.where(named, gates[:, :, None], 0.0), 1)
    earlier = jnp.arange(rows)[:, None] > jnp.arange(rows)[None, :]
    place = mm(earlier.astype(BF16), names.astype(BF16), 1, 0).astype(jnp.int32)
    place = jnp.where(names, place, -1)
    hot = jnp.argmax(jnp.sum(names.astype(jnp.int32), 0)).astype(jnp.int32)
    spot = (((place >> 3) - quarter) & 3) * 8 + (place & 7)
    spot = jnp.where((place >= 0) & (place < cap), spot, -1)
    to_send = dispatch(spot.T, weight.T, tokens, d_mixed)
    received = exchange(to_send.reshape(groups, cap, 2 * width))

    hit = spot[:, :, None] == jnp.arange(cap, dtype=jnp.int32)[None, None, :]
    gate_map = jnp.where(hit, weight[:, :, None], 0.0).reshape(rows, groups * cap)
    collect = jnp.concatenate(
        [*two_parts(gate_map), hit.astype(BF16).reshape(rows, groups * cap)], 0
    )
    hit_late = place.T[:, None, :] == jnp.arange(cap, 2 * cap, dtype=jnp.int32)[None, :, None]
    choose_late = jnp.any(hit_late, 0).astype(BF16)
    gate_late = jnp.sum(jnp.where(hit_late, weight.T[:, None, :], 0.0), 0)

    x_late = mm(choose_late, tokens, 1, 0).astype(BF16)
    s_late = mm(choose_late, d_mixed, 1, 0) * jnp.sum(gate_late, 1, keepdims=True)
    hot_send = jnp.concatenate(
        [
            spread(jnp.concatenate([x_late, s_late.astype(BF16)], 0)),
            split(up_home.T),
            split(down_home),
        ],
        1,
    )
    hot_send, received, collect = after(hot_send, received, collect)
    hot_got = exchange_in_plane(hot_send)

    received = received.reshape(2, near, 4, 8, 2 * width)

    def by_quarter(which):
        return pick(received, which).transpose(1, 0, 2, 3).reshape(512, 2 * width)

    own_rows, other_rows = by_quarter(core), by_quarter(1 - core)
    pre, back, *started = sum_over_features(own_rows, other_rows, up_home, down_home)
    hot_got = after(hot_got, *started)[0]
    logistic = jax.nn.sigmoid(pre)
    share = jnp.stack(
        [pre * logistic, back * logistic * (1.0 + pre * (1.0 - logistic))], 0
    ).astype(BF16)

    x_hot = flat(hot_got[:, :cap])
    s_hot = flat(hot_got[:, cap : 2 * cap])
    slices = pick(hot_got, hot % near)[2 * cap :]
    slices = jnp.where(hot // near == plane, slices, partner(slices))
    up_slice, down_slice = slices[:64], slices[64:]
    parts_hot = jnp.stack([mm(up_slice, x_hot, 1, 1), mm(down_slice, s_hot, 1, 1)], 0)
    sums_hot = sum_small(parts_hot.astype(BF16), pre, back)
    logistic_hot = jax.nn.sigmoid(sums_hot[0])
    hidden_hot = sums_hot[0] * logistic_hot
    grad_hot = sums_hot[1] * logistic_hot * (1.0 + sums_hot[0] * (1.0 - logistic_hot))
    hidden_hot, grad_hot = both_cores(jnp.stack([hidden_hot, grad_hot], 0).astype(BF16))
    out_hot = mm(hidden_hot, down_slice, 0, 0).astype(BF16)
    in_hot = mm(grad_hot, up_slice, 0, 0).astype(BF16)
    weight_grads = jnp.concatenate(
        [mm(hidden_hot, s_hot, 1, 0), mm(grad_hot, x_hot, 1, 0)], 0
    ).astype(BF16)
    share, weight_grads = after(share, weight_grads)
    weight_grads = add16(weight_grads, partner(weight_grads))
    hot_back = jnp.concatenate([split(out_hot), split(in_hot), spread(weight_grads)], 1)
    pieces, used, hot_back = all_blocks(
        share, hot_back, lambda pairs: finish(pairs, down_home, up_home)
    )
    hot_home = exchange_in_plane(hot_back)
    own_near, own_far, other_near, other_far = used

    def by_source(near_rows, far_rows):
        rows_out = jnp.concatenate([near_rows[:256], far_rows, near_rows[256:]], 0)
        return rows_out.reshape(4, near, 8, 2 * width).transpose(1, 0, 2, 3)

    own_out, other_out = by_source(own_near, own_far), by_source(other_near, other_far)
    out_rows = jnp.stack(
        [jnp.where(core == 0, own_out, other_out), jnp.where(core == 0, other_out, own_out)], 0
    )
    out_rows, hot_home, *pieces = after(out_rows, hot_home, *pieces)
    table = flat(exchange(out_rows.reshape(groups, cap, 2 * width)))

    out_late = jnp.sum(hot_home[:, :cap].astype(F32), 0).astype(BF16)
    in_late = jnp.sum(hot_home[:, cap : 2 * cap].astype(F32), 0).astype(BF16)
    is_hot = me == hot
    down_extra = jnp.where(is_hot, flat(hot_home[:, 2 * cap : 2 * cap + 64]), 0)
    up_extra = jnp.where(is_hot, flat(hot_home[:, 2 * cap + 64 :]), 0).T
    units = jnp.concatenate([ordered(pieces[0], pieces[1]), ordered(pieces[2], pieces[3])], 0)
    hidden, grad_pre = units[:, 0].reshape(1024, 1024), units[:, 1].reshape(1024, 1024)
    rows_in = jnp.concatenate([own_rows, other_rows], 0)
    grad_up = mm(rows_in[:, :width], grad_pre, 0, 0) + up_extra.astype(F32)
    grad_down = mm(hidden, rows_in[:, width:], 0, 0) + down_extra.astype(F32)
    high_late, low_late = two_parts(gate_late)
    mixed_late = mm(high_late, out_late, 0, 0) + mm(low_late, out_late, 0, 0)
    tokens_late = mm(choose_late, in_late, 0, 0)

    mixed, d_tokens = combine(collect, table, mixed_late, tokens_late)
    return (
        mixed,
        d_tokens,
        grad_up.astype(BF16)[None],
        grad_down.astype(BF16)[None],
    )


def solution(mesh):
    in_specs = (
        P("expert", "dp"),
        P("expert", None),
        P("expert", None),
        P("expert", "dp"),
        P("expert", "dp", None),
        P("expert", None, "dp"),
    )
    out_specs = (
        P("expert", "dp"),
        P("expert", "dp"),
        P("expert", "dp", None),
        P("expert", None, "dp"),
    )
    return jax.shard_map(
        per_device, mesh=mesh, in_specs=in_specs, out_specs=out_specs, check_vma=False
    )
```
